32 devices in a mesh: seq: 8 (over y, x, core), grp: 4 (over z).
Axes of the slice: x: 2, y: 2, z: 4, core: 2. Of those that a mesh axis runs over, the one named last changes fastest.
Arguments:
- prompt_latent: bfloat16 [4, 8, 256, 576], P('grp', None, 'seq'), may hold values from -6 to 6
- lengths: int32 [4, 8], P('grp'), may hold values from 1 to 256, 1024 in all within a row
- assign: int32 [4, 8], P('grp'), may hold values from 0 to 7, each once within a row
- prefix_latent: bfloat16 [128, 576], P(('seq', 'grp')), may hold values from -6 to 6
- queries: bfloat16 [4, 8, 4, 128, 576], P('grp', 'seq'), may hold values from -16 to 16
- new_latent: bfloat16 [4, 8, 4, 576], P('grp', 'seq'), may hold values from -6 to 6
Outputs:
- attended: bfloat16 [4, 8, 4, 128, 512], P('grp', 'seq')
The draws below stay inside these ranges and needn't reach their ends.
Inputs may be any that keep to these rules, and one draw needn't show every extreme that they name: `lengths`: the 8 prompts of a group hold 1024 tokens together, and in every group one prompt has exactly 256. `assign`: each row of a group names each of its 8 prompts once.
All inputs are finite; a program needn't handle non-finite values.
Results may differ from the reference program's by a relative error of at most 0.0043.
Values may be sent and summed in bfloat16 or wider, within the bound.
A program may use at most 64 MiB of HBM per device.

```python
import math
import jax
import jax.numpy as jnp
import numpy as np
from jax import lax

H = 128
LAT = 512
KV = 576
STEPS = 4
LMAX = 256
PREFIX = 128
N_SEQ = 8
N_GRP = 4


def draw_prefix_latent(key, part):
    key = jax.random.fold_in(key, 11)
    drawn = jnp.clip(jax.random.normal(key, (PREFIX, KV), jnp.float32), -6.0, 6.0)
    return drawn.astype(jnp.bfloat16)


def draw_queries(key, part):
    key = jax.random.fold_in(key, 23)
    array_shape = (N_GRP, N_SEQ, STEPS, H, KV)
    drawn = jnp.clip(3.0 * jax.random.normal(key, array_shape, jnp.float32), -16.0, 16.0)
    return drawn.astype(jnp.bfloat16)


def block_scale(key, shape, pieces, least, high):
    def one(dim, shards_of):
        steps = jax.random.uniform(jax.random.fold_in(jax.random.fold_in(key, 6), dim), (shards_of,), jnp.float32, least / len(pieces), high / len(pieces))
        return jnp.repeat(jnp.exp(steps), shape[dim] // shards_of).reshape((-1,) + (1,) * (len(shape) - dim - 1))

    loudness = one(*pieces[0])
    for cut in pieces[1:]:
        loudness = loudness * one(*cut)
    return loudness


def length_profile(number_of, total, bound, lean):
    loads = [(1 << 20) // math.isqrt(grade ** lean) + 1 for grade in range(2, number_of + 1)]
    surplus, counts = total - bound - (number_of - 1), [1] * (number_of - 1)
    while surplus > 0:
        movable = [i for i in range(number_of - 1) if counts[i] < bound]
        pool, left = sum([loads[i] for i in movable]), surplus
        for i in movable:
            more = min(bound - counts[i], max(1, left * loads[i] // pool), surplus)
            counts[i] = counts[i] + more
            surplus = surplus - more
    return np.array([bound] + counts)


def ragged_sizes(rng, number_of, total, bound, lean):
    if number_of == 2:
        one = jax.random.randint(rng, (), max(1, total - bound), min(bound, total - 1) + 1)
        return jnp.stack([one, total - one])
    tallies = jnp.asarray(length_profile(number_of, total, bound, lean), jnp.int32)
    pairs = (number_of - 1) // 2
    donor, receiver = tallies[1:1 + 2 * pairs:2], tallies[2:2 + 2 * pairs:2]
    room = jnp.minimum(donor - 1, bound - receiver)
    moved = jax.random.randint(jax.random.fold_in(rng, 1), (pairs,), 0, 1 << 20) % (room + 1)
    tallies = tallies.at[1:1 + 2 * pairs:2].set(donor - moved).at[2:2 + 2 * pairs:2].set(receiver + moved)
    return tallies[jax.random.permutation(jax.random.fold_in(rng, 2), number_of)]


def scatter_about(own_key, extent, width, reach, cuts=(), held_as=jnp.bfloat16):
    values = width * jax.random.normal(own_key, extent, jnp.float32)
    if cuts:
        values = values * block_scale(own_key, extent, cuts, -0.22, 0.18)
    return jnp.clip(values, -reach, reach).astype(held_as)


def setup_inputs(seed: int = 0) -> dict:
    splits = jax.random.split(jax.random.key(seed), 7)
    prompt_latent = scatter_about(splits[0], (N_GRP, N_SEQ, LMAX, KV), 1.0, 6.0, ((0, 4), (2, 8)))
    lengths = jax.vmap(lambda own: ragged_sizes(own, N_SEQ, N_SEQ * LMAX // 2, LMAX, 2))(jax.random.split(splits[1], N_GRP)).reshape((N_GRP, N_SEQ)).astype(jnp.int32)
    assign = jax.vmap(lambda own: jax.random.permutation(own, N_SEQ))(jax.random.split(splits[2], N_GRP)).reshape((N_GRP, N_SEQ)).astype(jnp.int32)
    prefix_latent = draw_prefix_latent(jax.random.fold_in(splits[6], 71), 0)
    queries = draw_queries(jax.random.fold_in(splits[6], 71), 0)
    new_latent = scatter_about(splits[5], (N_GRP, N_SEQ, STEPS, KV), 1.0, 6.0, ((0, 4), (1, 8)))
    return dict(prompt_latent=prompt_latent, lengths=lengths, assign=assign, prefix_latent=prefix_latent, queries=queries, new_latent=new_latent)


SCALE = 192.0 ** -0.5


def rotate(rotary, position):
    half_width = rotary.shape[-1] // 2
    frequency = 10000.0 ** (-(jnp.arange(half_width).astype(jnp.float32)) / half_width)
    angles = position[..., None].astype(jnp.float32) * frequency
    lower_part = rotary[..., :half_width].astype(jnp.float32)
    upper_part = rotary[..., half_width:].astype(jnp.float32)
    cosine = jnp.cos(angles)
    sine = jnp.sin(angles)
    return jnp.concatenate([lower_part * cosine - upper_part * sine, lower_part * sine + upper_part * cosine], -1)


def attend(query_block, fresh, own_cache, prefix_latent, own_length):
    step_ids = jnp.arange(STEPS, dtype=jnp.int32)
    position = PREFIX + own_length + step_ids
    query_rot = rotate(query_block[..., LAT:], position[:, None]).astype(jnp.bfloat16)
    query_rows = jnp.concatenate([query_block[..., :LAT], query_rot], -1).reshape(STEPS * H, -1)
    fresh_rot = rotate(fresh[:, LAT:], position).astype(jnp.bfloat16)
    fresh_rows = jnp.concatenate([fresh[:, :LAT], fresh_rot], -1)
    key_rows = jnp.concatenate([prefix_latent, own_cache, fresh_rows], 0)
    cache_len = own_cache.shape[0]
    column = jnp.arange(key_rows.shape[0], dtype=jnp.int32)
    row_step = jnp.arange(STEPS * H, dtype=jnp.int32) // H
    early_mask = column < PREFIX + own_length
    fresh_mask = (column[None, :] - PREFIX - cache_len) <= row_step[:, None]
    live_mask = jnp.where(column[None, :] >= PREFIX + cache_len, fresh_mask, early_mask[None, :])
    scores = jnp.dot(query_rows, key_rows.T, preferred_element_type=jnp.float32) * SCALE
    scores = jnp.where(live_mask, scores, -jnp.inf)
    top_score = jnp.max(scores, -1, keepdims=True)
    expo = jnp.exp(scores - top_score)
    weights = expo.astype(jnp.bfloat16)
    numer = jnp.dot(weights, key_rows[:, :LAT], preferred_element_type=jnp.float32)
    denom = jnp.sum(expo, -1, keepdims=True)
    return (numer / denom).astype(jnp.bfloat16).reshape(STEPS, H, LAT)


def reference(prompt_latent, lengths, assign, prefix_latent, queries, new_latent):
    group_count, owner_count = assign.shape
    group_ids = jnp.repeat(jnp.arange(group_count, dtype=jnp.int32), owner_count)
    owner_ids = jnp.tile(jnp.arange(owner_count, dtype=jnp.int32), group_count)

    def one_request(id_pair):
        grp_index = id_pair[0]
        own_index = id_pair[1]
        prompt_id = assign[grp_index, own_index]
        own_length = lengths[grp_index, prompt_id]
        own_cache = prompt_latent[grp_index, prompt_id]
        return attend(queries[grp_index, own_index], new_latent[grp_index, own_index], own_cache, prefix_latent, own_length)

    results = lax.map(one_request, jnp.stack([group_ids, owner_ids], 1))
    return results.reshape(group_count, owner_count, STEPS, H, LAT)
```

```python
import functools
import math

import jax
import jax.numpy as jnp
from jax import lax
from jax.experimental import pallas as pl
from jax.experimental.pallas import tpu as pltpu
from jax.sharding import PartitionSpec as P

LAT = 512
SCALE = 192.0 ** (-0.5)
LOG2E = math.log2(math.e)
MESH = pl.DeviceIdType.MESH
CHUNK = 256


def half_swap(x):
    half = x.shape[-1] // 2
    return jnp.concatenate([x[:, half:], x[:, :half]], -1)


def kernel(
    n_seq, n_grp, steps, heads,
    lengths_hbm, assign_hbm, prompt_hbm, prefix_hbm, query_hbm, fresh_hbm,
    out_hbm,
    lengths_s, assign_s, prompt_v, outgoing, arrived, piece_v, pieces, shared, query_v, fresh_v, out_v,
    load_sem, out_sem, block_send, block_recv, piece_send, piece_recv, plane_send, plane_recv,
):
    me = lax.axis_index("seq")
    my_grp = lax.axis_index("grp")
    block = prompt_v.shape[1]
    piece = piece_v.shape[0]
    plane = n_seq * piece
    prefix_len = n_grp * plane
    rows = steps * heads
    width = query_v.shape[1]

    barrier = pltpu.get_barrier_semaphore()
    for k in range(1, n_seq):
        pl.semaphore_signal(barrier, inc=1, device_id={"seq": lax.rem(me + k, n_seq)}, device_id_type=MESH)
    for k in range(1, n_grp):
        pl.semaphore_signal(barrier, inc=1, device_id={"grp": lax.rem(my_grp + k, n_grp)}, device_id_type=MESH)

    loads = [
        pltpu.make_async_copy(src, dst, load_sem.at[i])
        for i, (src, dst) in enumerate([
            (prefix_hbm, piece_v),
            (assign_hbm, assign_s),
            (lengths_hbm, lengths_s),
            (prompt_hbm, prompt_v),
            (fresh_hbm, fresh_v),
            (query_hbm, query_v),
        ])
    ]
    for load in loads:
        load.start()
    prefix_load, assign_load, lengths_load, prompt_load, fresh_load, query_load = loads

    prefix_load.wait()
    pl.semaphore_wait(barrier, n_seq - 1 + n_grp - 1)

    def piece_copy(peer, slot):
        return pltpu.make_async_remote_copy(
            src_ref=piece_v, dst_ref=pieces.at[slot], send_sem=piece_send.at[peer], recv_sem=piece_recv.at[slot],
            device_id={"seq": peer}, device_id_type=MESH,
        )

    for k in range(1, n_seq):
        piece_copy(lax.rem(me + k, n_seq), me).start()

    assign_load.wait()
    prompt_load.wait()

    def block_copy(peer, slot):
        return pltpu.make_async_remote_copy(
            src_ref=outgoing.at[peer], dst_ref=arrived.at[pl.ds(pl.multiple_of(slot * block, block), block)],
            send_sem=block_send.at[peer], recv_sem=block_recv.at[slot],
            device_id={"seq": peer}, device_id_type=MESH,
        )

    for k in range(1, n_seq):
        peer = lax.rem(me + k, n_seq)
        outgoing[peer] = prompt_v[assign_s[0, peer]]
        block_copy(peer, me).start()
    own_id = assign_s[0, me]
    arrived[pl.ds(pl.multiple_of(me * block, block), block)] = prompt_v[own_id]

    lengths_load.wait()
    own_length = lengths_s[0, own_id]
    rotary = width - LAT
    half = rotary // 2
    lane = lax.broadcasted_iota(jnp.int32, (8, rotary), 1)
    row = lax.broadcasted_iota(jnp.int32, (8, rotary), 0)
    lane_half = jnp.where(lane >= half, lane - half, lane)
    frequency = jnp.exp(lane_half.astype(jnp.float32) * (-math.log(10000.0) / half))
    angles = (prefix_len + own_length + row).astype(jnp.float32) * frequency
    cosine = jnp.cos(angles)
    sine = jnp.sin(angles)
    sine = jnp.where(lane >= half, sine, -sine)

    fresh_load.wait()
    fresh = fresh_v[...].astype(jnp.float32)
    fresh_rot = fresh[:, LAT:] * cosine[:steps] + half_swap(fresh[:, LAT:]) * sine[:steps]
    fresh_rows = jnp.concatenate([fresh[:, :LAT], fresh_rot], -1)
    fresh_rows = jnp.concatenate([fresh_rows, jnp.zeros((16 - steps, width), jnp.float32)], 0)
    shared[pl.ds(prefix_len, 16)] = fresh_rows.astype(jnp.bfloat16)

    query_load.wait()
    for t in range(steps):
        x = query_v[pl.ds(t * heads, heads), LAT:].astype(jnp.float32)
        turned = x * cosine[t:t + 1] + half_swap(x) * sine[t:t + 1]
        query_v[pl.ds(t * heads, heads), LAT:] = turned.astype(jnp.bfloat16)

    pieces[me] = piece_v[...]
    for k in range(1, n_seq):
        slot = lax.rem(me + k, n_seq)
        piece_copy(slot, slot).wait_recv()
    plane_rows = jnp.concatenate([pieces[i].astype(jnp.float32) for i in range(n_seq)], 0)
    shared[pl.ds(pl.multiple_of(my_grp * plane, plane), plane)] = plane_rows.astype(jnp.bfloat16)

    def plane_copy(peer, slot):
        here = pl.ds(pl.multiple_of(slot * plane, plane), plane)
        return pltpu.make_async_remote_copy(
            src_ref=shared.at[here], dst_ref=shared.at[here], send_sem=plane_send.at[peer], recv_sem=plane_recv.at[slot],
            device_id={"grp": peer}, device_id_type=MESH,
        )

    for k in range(1, n_grp):
        plane_copy(lax.rem(my_grp + k, n_grp), my_grp).start()
    for k in range(1, n_grp):
        slot = lax.rem(my_grp + k, n_grp)
        plane_copy(slot, slot).wait_recv()

    def score(query, keys):
        return lax.dot_general(query, keys, (((1,), (1,)), ((), ())), preferred_element_type=jnp.float32)

    def attend(s, top, keys):
        e = jnp.exp2((s - top) * (SCALE * LOG2E))
        total = jnp.sum(e, -1, keepdims=True)
        return total, jnp.dot(e.astype(jnp.bfloat16), keys, preferred_element_type=jnp.float32)

    starts = range(0, rows, CHUNK)
    state = []
    for start in starts:
        query = query_v[pl.ds(start, CHUNK)]
        s = score(query, shared[...])
        column = lax.broadcasted_iota(jnp.int32, s.shape, 1)
        step = (start + lax.broadcasted_iota(jnp.int32, s.shape, 0)) // heads
        s = jnp.where(column - prefix_len <= step, s, -jnp.inf)
        top = jnp.max(s, -1, keepdims=True)
        total, acc = attend(s, top, shared[:, :LAT])
        state.append((top, total, acc))

    for k in range(1, n_seq):
        slot = lax.rem(me + k, n_seq)
        block_copy(slot, slot).wait_recv()

    stores = []
    for i, start in enumerate(starts):
        top, total, acc = state[i]
        query = query_v[pl.ds(start, CHUNK)]
        s = score(query, arrived[...])
        column = lax.broadcasted_iota(jnp.int32, s.shape, 1)
        s = jnp.where(column < own_length, s, -jnp.inf)
        new_top = jnp.maximum(top, jnp.max(s, -1, keepdims=True))
        factor = jnp.exp2((top - new_top) * (SCALE * LOG2E))
        more, part = attend(s, new_top, arrived[:, :LAT])
        total = total * factor + more
        result = (acc * factor + part) / total
        out_v[pl.ds(start, CHUNK)] = result.astype(jnp.bfloat16)
        here = pl.ds(start, CHUNK)
        store = pltpu.make_async_copy(out_v.at[here], out_hbm.at[here], out_sem.at[i])
        store.start()
        stores.append(store)

    for k in range(1, n_seq):
        peer = lax.rem(me + k, n_seq)
        piece_copy(peer, me).wait_send()
        block_copy(peer, me).wait_send()
    for k in range(1, n_grp):
        plane_copy(lax.rem(my_grp + k, n_grp), my_grp).wait_send()
    for store in stores:
        store.wait()


def shards(prompt_latent, lengths, assign, prefix_latent, queries, new_latent):
    n_seq, n_grp = lax.axis_size("seq"), lax.axis_size("grp")
    prompt = prompt_latent[0]
    prompts, block, width = prompt.shape
    piece = prefix_latent.shape[0]
    steps, heads = queries.shape[2:4]
    rows = steps * heads
    prefix_len = n_seq * n_grp * piece
    bf16 = jnp.bfloat16
    dma = pltpu.SemaphoreType.DMA
    out = pl.pallas_call(
        functools.partial(kernel, n_seq, n_grp, steps, heads),
        out_shape=jax.ShapeDtypeStruct((rows, LAT), bf16),
        in_specs=[pl.BlockSpec(memory_space=pl.ANY)] * 6,
        out_specs=pl.BlockSpec(memory_space=pl.ANY),
        scratch_shapes=[
            pltpu.SMEM(lengths.shape, jnp.int32),
            pltpu.SMEM(assign.shape, jnp.int32),
            pltpu.VMEM(prompt.shape, bf16),
            pltpu.VMEM((n_seq, block, width), bf16),
            pltpu.VMEM((n_seq * block, width), bf16),
            pltpu.VMEM((piece, width), bf16),
            pltpu.VMEM((n_seq, piece, width), bf16),
            pltpu.VMEM((prefix_len + 16, width), bf16),
            pltpu.VMEM((rows, width), bf16),
            pltpu.VMEM((steps, width), bf16),
            pltpu.VMEM((rows, LAT), bf16),
            dma((6,)),
            dma((rows // CHUNK,)),
            dma((n_seq,)), dma((n_seq,)),
            dma((n_seq,)), dma((n_seq,)),
            dma((n_grp,)), dma((n_grp,)),
        ],
        compiler_params=pltpu.CompilerParams(
            collective_id=0, has_side_effects=True, vmem_limit_bytes=48 * 1024 * 1024
        ),
    )(lengths, assign, prompt, prefix_latent, queries.reshape(rows, width), new_latent[0, 0])
    return out.reshape(1, 1, steps, heads, LAT)


def solution(mesh):
    placed = (
        P("grp", None, "seq", None),
        P("grp", None),
        P("grp", None),
        P(("seq", "grp"), None),
        P("grp", "seq", None, None, None),
        P("grp", "seq", None, None),
    )
    return jax.shard_map(
        shards,
        mesh=mesh,
        in_specs=placed,
        out_specs=P("grp", "seq", None, None, None),
        check_vma=False,
    )
```

```python
import functools
import math

import jax
import jax.numpy as jnp
from jax import lax
from jax.experimental import pallas as pl
from jax.experimental.pallas import tpu as pltpu
from jax.sharding import PartitionSpec as P

LAT = 512
SCALE = 192.0 ** (-0.5)
LOG2E = math.log2(math.e)
MESH = pl.DeviceIdType.MESH
CHUNK = 256


def half_swap(x):
    half = x.shape[-1] // 2
    return jnp.concatenate([x[:, half:], x[:, :half]], -1)


def kernel(
    n_seq, n_grp,
    lengths_hbm, assign_hbm, prompt_hbm, prefix_hbm, query_hbm, fresh_hbm,
    out_hbm,
    lengths_s, assign_s, prompt_v, outgoing, piece_v, pieces, keys, query_v, fresh_v, out_v,
    load_sem, query_sem, out_sem, block_send, block_recv, piece_send, piece_recv, plane_send, plane_recv,
):
    me = lax.axis_index("seq")
    my_grp = lax.axis_index("grp")
    steps, width, heads = query_hbm.shape
    block = prompt_v.shape[1]
    piece = piece_v.shape[0]
    plane = n_seq * piece
    prefix_len = n_grp * plane
    cache_len = n_seq * block
    rows = steps * heads

    barrier = pltpu.get_barrier_semaphore()
    for k in range(1, n_seq):
        pl.semaphore_signal(barrier, inc=1, device_id={"seq": lax.rem(me + k, n_seq)}, device_id_type=MESH)
    for k in range(1, n_grp):
        pl.semaphore_signal(barrier, inc=1, device_id={"grp": lax.rem(my_grp + k, n_grp)}, device_id_type=MESH)

    loads = [
        pltpu.make_async_copy(src, dst, load_sem.at[i])
        for i, (src, dst) in enumerate([
            (prefix_hbm, piece_v),
            (assign_hbm, assign_s),
            (prompt_hbm, prompt_v),
            (lengths_hbm, lengths_s),
            (fresh_hbm, fresh_v),
        ])
    ]
    query_loads = [
        pltpu.make_async_copy(query_hbm.at[t], query_v.at[:, pl.ds(t * heads, heads)], query_sem.at[t])
        for t in range(steps)
    ]
    for load in loads + query_loads:
        load.start()
    prefix_load, assign_load, prompt_load, lengths_load, fresh_load = loads

    prefix_load.wait()
    pl.semaphore_wait(barrier, n_seq - 1 + n_grp - 1)

    def piece_copy(peer, slot):
        return pltpu.make_async_remote_copy(
            src_ref=piece_v, dst_ref=pieces.at[slot], send_sem=piece_send.at[peer], recv_sem=piece_recv.at[slot],
            device_id={"seq": peer}, device_id_type=MESH,
        )

    for k in range(1, n_seq):
        piece_copy(lax.rem(me + k, n_seq), me).start()

    assign_load.wait()
    prompt_load.wait()

    def block_copy(peer, slot):
        return pltpu.make_async_remote_copy(
            src_ref=outgoing.at[peer], dst_ref=keys.at[pl.ds(pl.multiple_of(slot * block, block), block)],
            send_sem=block_send.at[peer], recv_sem=block_recv.at[slot],
            device_id={"seq": peer}, device_id_type=MESH,
        )

    for k in range(1, n_seq):
        peer = lax.rem(me + k, n_seq)
        outgoing[peer] = prompt_v[assign_s[0, peer]]
        block_copy(peer, me).start()
    own_id = assign_s[0, me]
    keys[pl.ds(pl.multiple_of(me * block, block), block)] = prompt_v[own_id]

    pieces[me] = piece_v[...]
    for k in range(1, n_seq):
        slot = lax.rem(me + k, n_seq)
        piece_copy(slot, slot).wait_recv()
    plane_rows = jnp.concatenate([pieces[i].astype(jnp.float32) for i in range(n_seq)], 0)
    keys[pl.ds(pl.multiple_of(cache_len + my_grp * plane, plane), plane)] = plane_rows.astype(jnp.bfloat16)

    def plane_copy(peer, slot):
        here = pl.ds(pl.multiple_of(cache_len + slot * plane, plane), plane)
        return pltpu.make_async_remote_copy(
            src_ref=keys.at[here], dst_ref=keys.at[here], send_sem=plane_send.at[peer], recv_sem=plane_recv.at[slot],
            device_id={"grp": peer}, device_id_type=MESH,
        )

    for k in range(1, n_grp):
        plane_copy(lax.rem(my_grp + k, n_grp), my_grp).start()

    lengths_load.wait()
    own_length = lengths_s[0, own_id]
    rotary = width - LAT
    half = rotary // 2
    slope = -math.log(10000.0) / half
    lane = lax.broadcasted_iota(jnp.int32, (8, rotary), 1)
    row = lax.broadcasted_iota(jnp.int32, (8, rotary), 0)
    lane_half = jnp.where(lane >= half, lane - half, lane)
    angles = (prefix_len + own_length + row).astype(jnp.float32) * jnp.exp(lane_half.astype(jnp.float32) * slope)
    sine = jnp.sin(angles)
    sine = jnp.where(lane >= half, sine, -sine)[:steps]
    cosine = jnp.cos(angles)[:steps]
    fresh_load.wait()
    fresh = fresh_v[...].astype(jnp.float32)
    fresh_rot = fresh[:, LAT:] * cosine + half_swap(fresh[:, LAT:]) * sine
    fresh_rows = jnp.concatenate([fresh[:, :LAT], fresh_rot], -1)
    fresh_rows = jnp.concatenate([fresh_rows, jnp.zeros((16 - steps, width), jnp.float32)], 0)
    keys[pl.ds(cache_len + prefix_len, 16)] = fresh_rows.astype(jnp.bfloat16)

    lane = lax.broadcasted_iota(jnp.int32, (half, 128), 1)
    row = lax.broadcasted_iota(jnp.int32, (half, 128), 0)
    angles = (prefix_len + own_length + lane).astype(jnp.float32) * jnp.exp(row.astype(jnp.float32) * slope)
    cosine = jnp.cos(angles)
    sine = jnp.sin(angles)
    for t in range(steps):
        query_loads[t].wait()
        here = pl.ds(t * heads, heads)
        a = query_v[LAT:LAT + half, here].astype(jnp.float32)
        b = query_v[LAT + half:, here].astype(jnp.float32)
        c = jnp.broadcast_to(cosine[:, t:t + 1], a.shape)
        s = jnp.broadcast_to(sine[:, t:t + 1], a.shape)
        query_v[LAT:LAT + half, here] = (a * c - b * s).astype(jnp.bfloat16)
        query_v[LAT + half:, here] = (a * s + b * c).astype(jnp.bfloat16)

    for k in range(1, n_grp):
        slot = lax.rem(my_grp + k, n_grp)
        plane_copy(slot, slot).wait_recv()

    def score(first, count, here):
        return jnp.dot(keys[pl.ds(first, count)], query_v[:, here], preferred_element_type=jnp.float32)

    chunks = [pl.ds(start, CHUNK) for start in range(0, rows, CHUNK)]
    shared = []
    for i, here in enumerate(chunks):
        s = score(cache_len, prefix_len + 16, here)
        key = lax.broadcasted_iota(jnp.int32, s.shape, 0) - prefix_len
        step = (i * CHUNK + lax.broadcasted_iota(jnp.int32, s.shape, 1)) // heads
        shared.append(jnp.where(key <= step, s, -jnp.inf))

    for k in range(1, n_seq):
        slot = lax.rem(me + k, n_seq)
        block_copy(slot, slot).wait_recv()

    stores = []
    for i, here in enumerate(chunks):
        s = score(0, cache_len, here)
        s = jnp.where(lax.broadcasted_iota(jnp.int32, s.shape, 0) < own_length, s, -jnp.inf)
        s = jnp.concatenate([s, shared[i]], 0)
        top = jnp.max(s, 0, keepdims=True)
        e = jnp.exp2((s - top) * (SCALE * LOG2E))
        w = (e * (1.0 / jnp.sum(e, 0, keepdims=True))).astype(jnp.bfloat16)
        result = lax.dot_general(w, keys[:, :LAT], (((0,), (0,)), ((), ())), preferred_element_type=jnp.float32)
        out_v[here] = result.astype(jnp.bfloat16)
        store = pltpu.make_async_copy(out_v.at[here], out_hbm.at[here], out_sem.at[i])
        store.start()
        stores.append(store)

    for k in range(1, n_seq):
        peer = lax.rem(me + k, n_seq)
        piece_copy(peer, me).wait_send()
        block_copy(peer, me).wait_send()
    for k in range(1, n_grp):
        plane_copy(lax.rem(my_grp + k, n_grp), my_grp).wait_send()
    for store in stores:
        store.wait()


def shards(prompt_latent, lengths, assign, prefix_latent, queries, new_latent):
    n_seq, n_grp = lax.axis_size("seq"), lax.axis_size("grp")
    prompt = prompt_latent[0]
    prompts, block, width = prompt.shape
    piece = prefix_latent.shape[0]
    steps, heads = queries.shape[2:4]
    rows = steps * heads
    prefix_len = n_seq * n_grp * piece
    bf16 = jnp.bfloat16
    dma = pltpu.SemaphoreType.DMA
    out = pl.pallas_call(
        functools.partial(kernel, n_seq, n_grp),
        out_shape=jax.ShapeDtypeStruct((rows, LAT), bf16),
        in_specs=[pl.BlockSpec(memory_space=pl.ANY)] * 6,
        out_specs=pl.BlockSpec(memory_space=pl.ANY),
        scratch_shapes=[
            pltpu.SMEM(lengths.shape, jnp.int32),
            pltpu.SMEM(assign.shape, jnp.int32),
            pltpu.VMEM(prompt.shape, bf16),
            pltpu.VMEM((n_seq, block, width), bf16),
            pltpu.VMEM((piece, width), bf16),
            pltpu.VMEM((n_seq, piece, width), bf16),
            pltpu.VMEM((n_seq * block + prefix_len + 16, width), bf16),
            pltpu.VMEM((width, rows), bf16),
            pltpu.VMEM((steps, width), bf16),
            pltpu.VMEM((rows, LAT), bf16),
            dma((5,)),
            dma((steps,)),
            dma((rows // CHUNK,)),
            dma((n_seq,)), dma((n_seq,)),
            dma((n_seq,)), dma((n_seq,)),
            dma((n_grp,)), dma((n_grp,)),
        ],
        compiler_params=pltpu.CompilerParams(
            collective_id=0, has_side_effects=True, vmem_limit_bytes=60 * 1024 * 1024
        ),
    )(lengths, assign, prompt, prefix_latent, queries[0, 0].transpose(0, 2, 1), new_latent[0, 0])
    return out.reshape(1, 1, steps, heads, LAT)


def solution(mesh):
    placed = (
        P("grp", None, "seq", None),
        P("grp", None),
        P("grp", None),
        P(("seq", "grp"), None),
        P("grp", "seq", None, None, None),
        P("grp", "seq", None, None),
    )
    return jax.shard_map(
        shards,
        mesh=mesh,
        in_specs=placed,
        out_specs=P("grp", "seq", None, None, None),
        check_vma=False,
    )
```

```python
import functools
import math

import jax
import jax.numpy as jnp
from jax import lax
from jax.experimental import pallas as pl
from jax.experimental.pallas import tpu as pltpu
from jax.sharding import PartitionSpec as P

LAT = 512
SCALE = 192.0 ** (-0.5)
LOG2E = math.log2(math.e)
MESH = pl.DeviceIdType.MESH
CHUNK = 256


def half_swap(x):
    half = x.shape[-1] // 2
    return jnp.concatenate([x[:, half:], x[:, :half]], -1)


def kernel(
    n_seq, n_grp,
    lengths_hbm, assign_hbm, prompt_hbm, prefix_hbm, query_hbm, fresh_hbm,
    out_v,
    lengths_s, assign_s, prompt_v, outgoing, piece_v, pieces, keys, query_v, fresh_v,
    load_sem, query_sem, block_send, block_recv, piece_send, piece_recv, plane_send, plane_recv,
):
    me = lax.axis_index("seq")
    my_grp = lax.axis_index("grp")
    steps, width, heads = query_hbm.shape
    block = prompt_v.shape[1]
    piece = piece_v.shape[0]
    plane = n_seq * piece
    prefix_len = n_grp * plane
    cache_len = n_seq * block
    rows = steps * heads

    barrier = pltpu.get_barrier_semaphore()
    loads = [
        pltpu.make_async_copy(src, dst, load_sem.at[i])
        for i, (src, dst) in enumerate([
            (prefix_hbm, piece_v),
            (assign_hbm, assign_s),
            (prompt_hbm, prompt_v),
            (lengths_hbm, lengths_s),
            (fresh_hbm, fresh_v),
        ])
    ]
    query_loads = [
        pltpu.make_async_copy(query_hbm.at[t], query_v.at[:, pl.ds(t * heads, heads)], query_sem.at[t])
        for t in range(steps)
    ]
    for load in loads + query_loads:
        load.start()
    prefix_load, assign_load, prompt_load, lengths_load, fresh_load = loads

    for k in range(1, n_seq):
        pl.semaphore_signal(barrier, inc=1, device_id={"seq": lax.rem(me + k, n_seq)}, device_id_type=MESH)
    for k in range(1, n_grp):
        pl.semaphore_signal(barrier, inc=1, device_id={"grp": lax.rem(my_grp + k, n_grp)}, device_id_type=MESH)

    prefix_load.wait()
    pl.semaphore_wait(barrier, n_seq - 1 + n_grp - 1)

    def piece_copy(peer, slot):
        return pltpu.make_async_remote_copy(
            src_ref=piece_v, dst_ref=pieces.at[slot], send_sem=piece_send.at[peer], recv_sem=piece_recv.at[slot],
            device_id={"seq": peer}, device_id_type=MESH,
        )

    for k in range(1, n_seq):
        piece_copy(lax.rem(me + k, n_seq), me).start()

    pieces[me] = piece_v[...]
    for k in range(1, n_seq):
        slot = lax.rem(me + k, n_seq)
        piece_copy(slot, slot).wait_recv()
    plane_rows = jnp.concatenate([pieces[i].astype(jnp.float32) for i in range(n_seq)], 0)
    keys[pl.ds(pl.multiple_of(cache_len + my_grp * plane, plane), plane)] = plane_rows.astype(jnp.bfloat16)

    def plane_copy(peer, slot):
        here = pl.ds(pl.multiple_of(cache_len + slot * plane, plane), plane)
        return pltpu.make_async_remote_copy(
            src_ref=keys.at[here], dst_ref=keys.at[here], send_sem=plane_send.at[peer], recv_sem=plane_recv.at[slot],
            device_id={"grp": peer}, device_id_type=MESH,
        )

    for k in range(1, n_grp):
        plane_copy(lax.rem(my_grp + k, n_grp), my_grp).start()

    assign_load.wait()
    prompt_load.wait()

    def block_copy(peer, slot):
        return pltpu.make_async_remote_copy(
            src_ref=outgoing.at[peer], dst_ref=keys.at[pl.ds(pl.multiple_of(slot * block, block), block)],
            send_sem=block_send.at[peer], recv_sem=block_recv.at[slot],
            device_id={"seq": peer}, device_id_type=MESH,
        )

    for k in range(1, n_seq):
        peer = lax.rem(me + k, n_seq)
        outgoing[peer] = prompt_v[assign_s[0, peer]]
        block_copy(peer, me).start()
    own_id = assign_s[0, me]
    keys[pl.ds(pl.multiple_of(me * block, block), block)] = prompt_v[own_id]

    lengths_load.wait()
    own_length = lengths_s[0, own_id]
    rotary = width - LAT
    half = rotary // 2
    slope = -math.log(10000.0) / half
    lane = lax.broadcasted_iota(jnp.int32, (8, rotary), 1)
    row = lax.broadcasted_iota(jnp.int32, (8, rotary), 0)
    lane_half = jnp.where(lane >= half, lane - half, lane)
    angles = (prefix_len + own_length + row).astype(jnp.float32) * jnp.exp(lane_half.astype(jnp.float32) * slope)
    sine = jnp.sin(angles)
    sine = jnp.where(lane >= half, sine, -sine)[:steps]
    cosine = jnp.cos(angles)[:steps]
    fresh_load.wait()
    fresh = fresh_v[...].astype(jnp.float32)
    fresh_rot = fresh[:, LAT:] * cosine + half_swap(fresh[:, LAT:]) * sine
    fresh_rows = jnp.concatenate([fresh[:, :LAT], fresh_rot], -1)
    fresh_rows = jnp.concatenate([fresh_rows, jnp.zeros((16 - steps, width), jnp.float32)], 0)
    keys[pl.ds(cache_len + prefix_len, 16)] = fresh_rows.astype(jnp.bfloat16)

    lane = lax.broadcasted_iota(jnp.int32, (half, 128), 1)
    row = lax.broadcasted_iota(jnp.int32, (half, 128), 0)
    angles = (prefix_len + own_length + lane).astype(jnp.float32) * jnp.exp(row.astype(jnp.float32) * slope)
    cosine = jnp.cos(angles)
    sine = jnp.sin(angles)
    for t in range(steps):
        query_loads[t].wait()
        here = pl.ds(t * heads, heads)
        a = query_v[LAT:LAT + half, here].astype(jnp.float32)
        b = query_v[LAT + half:, here].astype(jnp.float32)
        c = jnp.broadcast_to(cosine[:, t:t + 1], a.shape)
        s = jnp.broadcast_to(sine[:, t:t + 1], a.shape)
        query_v[LAT:LAT + half, here] = (a * c - b * s).astype(jnp.bfloat16)
        query_v[LAT + half:, here] = (a * s + b * c).astype(jnp.bfloat16)

    for k in range(1, n_grp):
        slot = lax.rem(my_grp + k, n_grp)
        plane_copy(slot, slot).wait_recv()

    def score(first, count, here):
        return jnp.dot(keys[pl.ds(first, count)], query_v[:, here], preferred_element_type=jnp.float32)

    chunks = [pl.ds(start, CHUNK) for start in range(0, rows, CHUNK)]
    shared = []
    for i, here in enumerate(chunks):
        s = score(cache_len, prefix_len + 16, here)
        key = lax.broadcasted_iota(jnp.int32, s.shape, 0) - prefix_len
        step = (i * CHUNK + lax.broadcasted_iota(jnp.int32, s.shape, 1)) // heads
        shared.append(jnp.where(key <= step, s, -jnp.inf))

    for k in range(1, n_seq):
        slot = lax.rem(me + k, n_seq)
        block_copy(slot, slot).wait_recv()

    for i, here in enumerate(chunks):
        s = score(0, cache_len, here)
        s = jnp.where(lax.broadcasted_iota(jnp.int32, s.shape, 0) < own_length, s, -jnp.inf)
        s = jnp.concatenate([s, shared[i]], 0)
        top = jnp.max(s, 0, keepdims=True)
        e = jnp.exp2((s - top) * (SCALE * LOG2E))
        total = jnp.broadcast_to(jnp.sum(e, 0, keepdims=True), (8, CHUNK)).T[:, :1]
        w = e.astype(jnp.bfloat16)
        result = lax.dot_general(w, keys[:, :LAT], (((0,), (0,)), ((), ())), preferred_element_type=jnp.float32)
        out_v[here] = (result * (1.0 / total)).astype(jnp.bfloat16)

    for k in range(1, n_seq):
        peer = lax.rem(me + k, n_seq)
        piece_copy(peer, me).wait_send()
        block_copy(peer, me).wait_send()
    for k in range(1, n_grp):
        plane_copy(lax.rem(my_grp + k, n_grp), my_grp).wait_send()


def shards(prompt_latent, lengths, assign, prefix_latent, queries, new_latent):
    n_seq, n_grp = lax.axis_size("seq"), lax.axis_size("grp")
    prompt = prompt_latent[0]
    prompts, block, width = prompt.shape
    piece = prefix_latent.shape[0]
    steps, heads = queries.shape[2:4]
    rows = steps * heads
    prefix_len = n_seq * n_grp * piece
    bf16 = jnp.bfloat16
    dma = pltpu.SemaphoreType.DMA
    out = pl.pallas_call(
        functools.partial(kernel, n_seq, n_grp),
        out_shape=pltpu.VMEM((rows, LAT), bf16),
        in_specs=[pl.BlockSpec(memory_space=pltpu.HBM)] * 6,
        out_specs=pl.BlockSpec(memory_space=pltpu.VMEM),
        scratch_shapes=[
            pltpu.SMEM(lengths.shape, jnp.int32),
            pltpu.SMEM(assign.shape, jnp.int32),
            pltpu.VMEM(prompt.shape, bf16),
            pltpu.VMEM((n_seq, block, width), bf16),
            pltpu.VMEM((piece, width), bf16),
            pltpu.VMEM((n_seq, piece, width), bf16),
            pltpu.VMEM((n_seq * block + prefix_len + 16, width), bf16),
            pltpu.VMEM((width, rows), bf16),
            pltpu.VMEM((steps, width), bf16),
            dma((5,)),
            dma((steps,)),
            dma((n_seq,)), dma((n_seq,)),
            dma((n_seq,)), dma((n_seq,)),
            dma((n_grp,)), dma((n_grp,)),
        ],
        compiler_params=pltpu.CompilerParams(
            collective_id=0, has_side_effects=True, vmem_limit_bytes=62 * 1024 * 1024
        ),
    )(lengths, assign, prompt, prefix_latent, queries[0, 0].transpose(0, 2, 1), new_latent[0, 0])
    return out.reshape(1, 1, steps, heads, LAT)


def solution(mesh):
    placed = (
        P("grp", None, "seq", None),
        P("grp", None),
        P("grp", None),
        P(("seq", "grp"), None),
        P("grp", "seq", None, None, None),
        P("grp", "seq", None, None),
    )
    return jax.shard_map(
        shards,
        mesh=mesh,
        in_specs=placed,
        out_specs=P("grp", "seq", None, None, None),
        check_vma=False,
    )
```

```python
import functools
import math

import jax
import jax.numpy as jnp
from jax import lax
from jax.experimental import pallas as pl
from jax.experimental.pallas import tpu as pltpu
from jax.sharding import PartitionSpec as P

LAT = 512
SCALE = 192.0 ** (-0.5)
LOG2E = math.log2(math.e)
MESH = pl.DeviceIdType.MESH
CHUNK = 256


def half_swap(x):
    half = x.shape[-1] // 2
    return jnp.concatenate([x[:, half:], x[:, :half]], -1)


def kernel(
    n_seq, n_grp,
    lengths_hbm, assign_hbm, prompt_hbm, prefix_hbm, query_hbm, fresh_hbm,
    out_v,
    lengths_s, assign_s, prompt_v, outgoing, piece_v, pieces, keys, query_v, fresh_v,
    load_sem, query_sem, block_send, block_recv, piece_send, piece_recv, plane_send, plane_recv,
):
    me = lax.axis_index("seq")
    my_grp = lax.axis_index("grp")
    steps, width, heads = query_hbm.shape
    block = prompt_v.shape[1]
    piece = piece_v.shape[0]
    plane = n_grp * piece
    prefix_len = n_seq * plane
    cache_len = n_seq * block
    rows = steps * heads

    barrier = pltpu.get_barrier_semaphore()
    loads = [
        pltpu.make_async_copy(src, dst, load_sem.at[i])
        for i, (src, dst) in enumerate([
            (prefix_hbm, piece_v),
            (assign_hbm, assign_s),
            (prompt_hbm, prompt_v),
            (lengths_hbm, lengths_s),
            (fresh_hbm, fresh_v),
        ])
    ]
    query_loads = [
        pltpu.make_async_copy(query_hbm.at[t], query_v.at[:, pl.ds(t * heads, heads)], query_sem.at[t])
        for t in range(steps)
    ]
    for load in loads + query_loads:
        load.start()
    prefix_load, assign_load, prompt_load, lengths_load, fresh_load = loads

    for k in range(1, n_grp):
        pl.semaphore_signal(barrier, inc=1, device_id={"grp": lax.rem(my_grp + k, n_grp)}, device_id_type=MESH)
    for k in range(1, n_seq):
        pl.semaphore_signal(barrier, inc=1, device_id={"seq": lax.rem(me + k, n_seq)}, device_id_type=MESH)

    prefix_load.wait()
    pl.semaphore_wait(barrier, n_seq - 1 + n_grp - 1)

    def piece_copy(peer, slot):
        return pltpu.make_async_remote_copy(
            src_ref=piece_v, dst_ref=pieces.at[slot], send_sem=piece_send.at[peer], recv_sem=piece_recv.at[slot],
            device_id={"grp": peer}, device_id_type=MESH,
        )

    for k in range(1, n_grp):
        piece_copy(lax.rem(my_grp + k, n_grp), my_grp).start()

    assign_load.wait()
    prompt_load.wait()
    for peer in range(n_seq):
        outgoing[peer] = prompt_v[assign_s[0, peer]]
    own_id = assign_s[0, me]
    keys[pl.ds(pl.multiple_of(me * block, block), block)] = prompt_v[own_id]

    def block_copy(peer, slot):
        return pltpu.make_async_remote_copy(
            src_ref=outgoing.at[peer], dst_ref=keys.at[pl.ds(pl.multiple_of(slot * block, block), block)],
            send_sem=block_send.at[peer], recv_sem=block_recv.at[slot],
            device_id={"seq": peer}, device_id_type=MESH,
        )

    for k in range(1, n_seq):
        peer = lax.rem(me + k, n_seq)
        block_copy(peer, me).start()
    pieces[my_grp] = piece_v[...]
    for k in range(1, n_grp):
        slot = lax.rem(my_grp + k, n_grp)
        piece_copy(slot, slot).wait_recv()
    plane_rows = jnp.concatenate([pieces[i].astype(jnp.float32) for i in range(n_grp)], 0)
    keys[pl.ds(pl.multiple_of(cache_len + me * plane, plane), plane)] = plane_rows.astype(jnp.bfloat16)

    def plane_copy(peer, slot):
        here = pl.ds(pl.multiple_of(cache_len + slot * plane, plane), plane)
        return pltpu.make_async_remote_copy(
            src_ref=keys.at[here], dst_ref=keys.at[here], send_sem=plane_send.at[peer], recv_sem=plane_recv.at[slot],
            device_id={"seq": peer}, device_id_type=MESH,
        )

    for k in range(1, n_seq):
        plane_copy(lax.rem(me + k, n_seq), me).start()

    lengths_load.wait()
    own_length = lengths_s[0, own_id]
    rotary = width - LAT
    half = rotary // 2
    slope = -math.log(10000.0) / half
    lane = lax.broadcasted_iota(jnp.int32, (8, rotary), 1)
    row = lax.broadcasted_iota(jnp.int32, (8, rotary), 0)
    lane_half = jnp.where(lane >= half, lane - half, lane)
    angles = (prefix_len + own_length + row).astype(jnp.float32) * jnp.exp(lane_half.astype(jnp.float32) * slope)
    sine = jnp.sin(angles)
    sine = jnp.where(lane >= half, sine, -sine)[:steps]
    cosine = jnp.cos(angles)[:steps]
    fresh_load.wait()
    fresh = fresh_v[...].astype(jnp.float32)
    fresh_rot = fresh[:, LAT:] * cosine + half_swap(fresh[:, LAT:]) * sine
    fresh_rows = jnp.concatenate([fresh[:, :LAT], fresh_rot], -1)
    fresh_rows = jnp.concatenate([fresh_rows, jnp.zeros((16 - steps, width), jnp.float32)], 0)
    keys[pl.ds(cache_len + prefix_len, 16)] = fresh_rows.astype(jnp.bfloat16)

    lane = lax.broadcasted_iota(jnp.int32, (half, 128), 1)
    row = lax.broadcasted_iota(jnp.int32, (half, 128), 0)
    angles = (prefix_len + own_length + lane).astype(jnp.float32) * jnp.exp(row.astype(jnp.float32) * slope)
    cosine = jnp.cos(angles)
    sine = jnp.sin(angles)
    for t in range(steps):
        query_loads[t].wait()
        here = pl.ds(t * heads, heads)
        a = query_v[LAT:LAT + half, here].astype(jnp.float32)
        b = query_v[LAT + half:, here].astype(jnp.float32)
        c = jnp.broadcast_to(cosine[:, t:t + 1], a.shape)
        s = jnp.broadcast_to(sine[:, t:t + 1], a.shape)
        query_v[LAT:LAT + half, here] = (a * c - b * s).astype(jnp.bfloat16)
        query_v[LAT + half:, here] = (a * s + b * c).astype(jnp.bfloat16)

    for k in range(1, n_seq):
        slot = lax.rem(me + k, n_seq)
        plane_copy(slot, slot).wait_recv()

    def score(first, count, here):
        return jnp.dot(keys[pl.ds(first, count)], query_v[:, here], preferred_element_type=jnp.float32)

    chunks = [pl.ds(start, CHUNK) for start in range(0, rows, CHUNK)]
    shared = []
    for i, here in enumerate(chunks):
        s = score(cache_len, prefix_len + 16, here)
        key = lax.broadcasted_iota(jnp.int32, s.shape, 0) - prefix_len
        step = (i * CHUNK + lax.broadcasted_iota(jnp.int32, s.shape, 1)) // heads
        shared.append(jnp.where(key <= step, s, -jnp.inf))

    for k in range(1, n_seq):
        slot = lax.rem(me + k, n_seq)
        block_copy(slot, slot).wait_recv()

    for i, here in enumerate(chunks):
        s = score(0, cache_len, here)
        s = jnp.where(lax.broadcasted_iota(jnp.int32, s.shape, 0) < own_length, s, -jnp.inf)
        s = jnp.concatenate([s, shared[i]], 0)
        top = jnp.max(s, 0, keepdims=True)
        e = jnp.exp2((s - top) * (SCALE * LOG2E))
        total = jnp.broadcast_to(jnp.sum(e, 0, keepdims=True), (8, CHUNK)).T[:, :1]
        w = e.astype(jnp.bfloat16)
        result = lax.dot_general(w, keys[:, :LAT], (((0,), (0,)), ((), ())), preferred_element_type=jnp.float32)
        out_v[here] = (result * (1.0 / total)).astype(jnp.bfloat16)

    for k in range(1, n_seq):
        peer = lax.rem(me + k, n_seq)
        plane_copy(peer, me).wait_send()
        block_copy(peer, me).wait_send()
    for k in range(1, n_grp):
        piece_copy(lax.rem(my_grp + k, n_grp), my_grp).wait_send()


def shards(prompt_latent, lengths, assign, prefix_latent, queries, new_latent):
    n_seq, n_grp = lax.axis_size("seq"), lax.axis_size("grp")
    prompt = prompt_latent[0]
    prompts, block, width = prompt.shape
    piece = prefix_latent.shape[0]
    steps, heads = queries.shape[2:4]
    rows = steps * heads
    prefix_len = n_seq * n_grp * piece
    bf16 = jnp.bfloat16
    dma = pltpu.SemaphoreType.DMA
    out = pl.pallas_call(
        functools.partial(kernel, n_seq, n_grp),
        out_shape=pltpu.VMEM((rows, LAT), bf16),
        in_specs=[pl.BlockSpec(memory_space=pltpu.HBM)] * 6,
        out_specs=pl.BlockSpec(memory_space=pltpu.VMEM),
        scratch_shapes=[
            pltpu.SMEM(lengths.shape, jnp.int32),
            pltpu.SMEM(assign.shape, jnp.int32),
            pltpu.VMEM(prompt.shape, bf16),
            pltpu.VMEM((n_seq, block, width), bf16),
            pltpu.VMEM((piece, width), bf16),
            pltpu.VMEM((n_grp, piece, width), bf16),
            pltpu.VMEM((n_seq * block + prefix_len + 16, width), bf16),
            pltpu.VMEM((width, rows), bf16),
            pltpu.VMEM((steps, width), bf16),
            dma((5,)),
            dma((steps,)),
            dma((n_seq,)), dma((n_seq,)),
            dma((n_grp,)), dma((n_grp,)),
            dma((n_seq,)), dma((n_seq,)),
        ],
        compiler_params=pltpu.CompilerParams(
            collective_id=0, has_side_effects=True, vmem_limit_bytes=62 * 1024 * 1024
        ),
    )(lengths, assign, prompt, prefix_latent, queries[0, 0].transpose(0, 2, 1), new_latent[0, 0])
    return out.reshape(1, 1, steps, heads, LAT)


def solution(mesh):
    placed = (
        P("grp", None, "seq", None),
        P("grp", None),
        P("grp", None),
        P(("seq", "grp"), None),
        P("grp", "seq", None, None, None),
        P("grp", "seq", None, None),
    )
    return jax.shard_map(
        shards,
        mesh=mesh,
        in_specs=placed,
        out_specs=P("grp", "seq", None, None, None),
        check_vma=False,
    )
```
